32 devices in a mesh: groups: 2 (over x), seq: 16 (over z, y, core).
Axes of the slice: x: 2, y: 2, z: 4, core: 2. Of those that a mesh axis runs over, the one named last changes fastest.
Arguments:
- tokens: bfloat16 [32768, 2048], P(('groups', 'seq')), parts along dimension 0, may hold values from -64 to 64, as said below
- gain_mix: float32 [2048], replicated, may hold values from 0.1 to 1.9
- gain_mlp: float32 [2048], replicated, may hold values from 0.1 to 1.9
- block_mix: bfloat16 [1024, 1024], replicated, may hold values from -0.1875 to 0.1875
- cross_mix: bfloat16 [16, 16], replicated, may hold values from -1.5 to 1.5
- w_in: bfloat16 [2048, 1024], P('seq'), may hold values from -0.25 to 0.25
- w_out: bfloat16 [4096, 512], P('seq'), may hold values from -0.1875 to 0.1875
Outputs:
- mixed: bfloat16 [32768, 2048], P(('groups', 'seq')), parts along dimension 0
The draws below stay inside these ranges and needn't reach their ends.
There are 2 independent parts, one for each index of `groups`. The reference program is written for one: setup_inputs(seed, part) draws one part's arguments, and reference() takes and returns one part's arrays. A program takes and returns all parts, laid end to end along the dimension named above; an argument that names none is the same for every part. Nothing has to cross between parts.
Inputs may be any that keep to these rules, and one draw needn't show every extreme that they name: `tokens`: activations with independent scales per channel and per position.
All inputs are finite; a program needn't handle non-finite values.
Results may differ from the reference program's by a relative error of at most 0.0085.
Values may be sent and summed in bfloat16 or wider, within the bound.
A program may use at most 128 MiB of HBM per device.

```python
import math
import jax
import jax.numpy as jnp
from jax import lax

D = 2048
FF = 4096
NCB = 4
BLK = 1024
LEN = 16384
B1 = 16


def draw_tokens(key, part):
    key_base, key_cols, key_rows = jax.random.split(key, 3)
    base = jnp.clip(jax.random.normal(key_base, (LEN, D), jnp.float32), -6.0, 6.0)
    columns = jnp.exp(jax.random.uniform(key_cols, (1, D), jnp.float32, math.log(0.32), math.log(3.2)))
    rowscale = jnp.exp(jax.random.uniform(key_rows, (LEN, 1), jnp.float32, math.log(0.32), math.log(3.2)))
    return (base * columns * rowscale).astype(jnp.bfloat16)


def steps_of(own_key, extent, cuts, smallest, largest):
    loudness = 1.0
    for axis_at, blocks in cuts:
        steps = jax.random.uniform(jax.random.fold_in(jax.random.fold_in(own_key, 6), axis_at), (blocks,), jnp.float32, smallest / len(cuts), largest / len(cuts))
        loudness = loudness * jnp.repeat(jnp.exp(steps), extent[axis_at] // blocks).reshape((-1,) + (1,) * (len(extent) - 1 - axis_at))
    return loudness


def noise(own_key, shape, width, most, shards=(), dtype=jnp.bfloat16):
    values = width * jax.random.normal(own_key, shape, jnp.float32)
    if shards:
        values = values * steps_of(own_key, shape, shards, -0.22, 0.18)
    return jnp.clip(values, -most, most).astype(dtype)


def setup_inputs(seed: int = 0, part: int = 0) -> dict:
    seeds = jax.random.split(jax.random.key(seed), 8)
    part_keys = jax.random.split(jax.random.fold_in(seeds[7], part), 8)
    return {
        "tokens": draw_tokens(jax.random.fold_in(jax.random.fold_in(seeds[7], part), 71), part),
        "gain_mix": jnp.clip(1.0 + 0.18 * jax.random.normal(seeds[1], (D,), jnp.float32), 0.1, 1.9),
        "gain_mlp": jnp.clip(1.0 + 0.18 * jax.random.normal(seeds[2], (D,), jnp.float32), 0.1, 1.9),
        "block_mix": noise(seeds[3], (BLK, BLK), BLK ** -0.5, 0.1875),
        "cross_mix": noise(seeds[4], (B1, B1), B1 ** -0.5, 1.5),
        "w_in": noise(seeds[5], (D, FF // NCB), (D // NCB) ** -0.5, 0.25, ((0, 16),)),
        "w_out": noise(seeds[6], (FF, D // NCB), (FF // NCB) ** -0.5, 0.1875, ((0, 16),)),
    }


def rms_scale(values, gain):
    mean_square = lax.optimization_barrier(jnp.mean(values * values, axis=-1, keepdims=True))
    return values * lax.rsqrt(mean_square + 1e-06) * gain

def reference(tokens, gain_mix, gain_mlp, block_mix, cross_mix, w_in, w_out):
    count = LEN // BLK
    normed = rms_scale(tokens.astype(jnp.float32), gain_mix).astype(jnp.bfloat16)
    blocks = normed.reshape(count, BLK, D)

    def first_factor(block):
        return jnp.dot(block_mix, block, preferred_element_type=jnp.float32).astype(jnp.bfloat16)
    within = lax.map(first_factor, blocks)
    across = jnp.dot(cross_mix, within.reshape(count, BLK * D), preferred_element_type=jnp.float32)
    across = across.astype(jnp.bfloat16).reshape(count, BLK, D)
    weight_in = w_in.reshape(NCB, D // NCB, FF // NCB).astype(jnp.float32)
    weight_out = w_out.reshape(NCB, FF // NCB, D // NCB).astype(jnp.float32)

    def tail(inputs):
        raw, normed_block, mixed_block = inputs
        gated = (raw.astype(jnp.float32) + normed_block.astype(jnp.float32) * mixed_block.astype(jnp.float32)).astype(jnp.bfloat16)
        inner = rms_scale(gated.astype(jnp.float32), gain_mlp).astype(jnp.bfloat16)
        hidden = jnp.einsum('rcd,cdf->rcf', inner.reshape(BLK, NCB, D // NCB).astype(jnp.float32), weight_in)
        hidden = jax.nn.gelu(hidden).astype(jnp.bfloat16)
        output = jnp.einsum('rcf,cfd->rcd', hidden.astype(jnp.float32), weight_out).reshape(BLK, D)
        return (gated.astype(jnp.float32) + output).astype(jnp.bfloat16)
    result = lax.map(tail, (tokens.reshape(count, BLK, D), blocks, across))
    return result.reshape(LEN, D)
```

```python
import jax
import jax.numpy as jnp
from jax import lax
from jax.experimental import pallas as pl
from jax.experimental.pallas import tpu as pltpu
from jax.sharding import PartitionSpec as P

NCB = 4
BLK = 1024
CHUNKS = 8
LANES = 128
SUB = 16
MESH = pl.DeviceIdType.MESH
BF16 = jnp.bfloat16
F32 = jnp.float32


def kernel(
    n, tokens, gain_mix, gain_mlp, block_mix, cross_mix, w_in, w_out, out,
    tok, normed, mat, win, wout, send1, got1, send2, got2, kron, gated, inner, result,
    load_sem, mat_sem, own_sem, line_send, line_recv, hop_send, hop_recv,
    s1, r1, s2, r2, out_sem,
):
    width = tokens.shape[1]
    part = BLK // CHUNKS
    col_groups = width // LANES
    row_groups = n // col_groups
    rows = part // row_groups
    line = n // 4
    x = lax.axis_index("groups")
    me = lax.axis_index("seq")
    at, lane = me // 4, me % 4
    y, core = lane // 2, lane % 2

    def rows_of(g):
        return pl.ds(pl.multiple_of(g * part, part), part)

    def load(g):
        return pltpu.make_async_copy(tokens.at[rows_of(g)], tok.at[rows_of(g)], load_sem.at[g])

    @pl.loop(0, CHUNKS)
    def _(g):
        load(g).start()

    load_mat = pltpu.make_async_copy(block_mix, mat, mat_sem)
    load_mat.start()

    barrier = pltpu.get_barrier_semaphore()

    @pl.loop(1, n)
    def _(k):
        pl.semaphore_signal(barrier, inc=1, device_id=(x, (me + k) % n), device_id_type=MESH)

    pl.semaphore_signal(barrier, inc=1, device_id=(1 - x, me), device_id_type=MESH)
    pl.semaphore_wait(barrier, n)

    def by_kind(fn):
        @pl.when(x == 0)
        def _():
            fn(w_in, win)

        @pl.when(x == 1)
        def _():
            fn(w_out, wout)

    def line_copy(full, t, way):
        shard = at - t if way == 0 else at + t
        to = at + 1 if way == 0 else at - 1
        return pltpu.make_async_remote_copy(
            src_ref=full.at[shard, lane], dst_ref=full.at[shard, lane],
            send_sem=line_send.at[way, t], recv_sem=line_recv.at[way, t],
            device_id=(x, to * 4 + lane), device_id_type=MESH,
        )

    def line_start(t):
        def go(_, full):
            @pl.when((at < line - 1) & (at - t >= 0))
            def _():
                line_copy(full, t, 0).start()

            @pl.when((at > 0) & (at + t <= line - 1))
            def _():
                line_copy(full, t, 1).start()
        by_kind(go)

    def line_arrived(t):
        def go(_, full):
            @pl.when(at - 1 - t >= 0)
            def _():
                block = full.at[at - 1 - t, lane]
                pltpu.make_async_copy(block, block, line_recv.at[0, t]).wait()

            @pl.when(at + 1 + t <= line - 1)
            def _():
                block = full.at[at + 1 + t, lane]
                pltpu.make_async_copy(block, block, line_recv.at[1, t]).wait()
        by_kind(go)

    def line_sent(t):
        def go(_, full):
            @pl.when((at < line - 1) & (at - t >= 0))
            def _():
                line_copy(full, t, 0).wait_send()

            @pl.when((at > 0) & (at + t <= line - 1))
            def _():
                line_copy(full, t, 1).wait_send()
        by_kind(go)

    def hop(full, which, slot, device):
        return pltpu.make_async_remote_copy(
            src_ref=full.at[:, which], dst_ref=full.at[:, which],
            send_sem=hop_send.at[slot], recv_sem=hop_recv.at[slot],
            device_id=device, device_id_type=MESH,
        )

    def arrived(full, which, slot):
        block = full.at[:, which]
        pltpu.make_async_copy(block, block, hop_recv.at[slot]).wait()

    over_y = (1 - y) * 2 + core
    over_c = y * 2 + 1 - core
    over_yc = (1 - y) * 2 + 1 - core
    peer_y = (x, at * 4 + over_y)
    peer_x = (1 - x, me)
    peer_c = (x, at * 4 + over_c)

    def own(shard, full):
        return pltpu.make_async_copy(shard, full.at[at, lane], own_sem)

    by_kind(lambda shard, full: own(shard, full).start())
    by_kind(lambda shard, full: own(shard, full).wait())
    line_start(0)

    big = n * SUB
    pick = (lax.broadcasted_iota(jnp.int32, (big, n), 0) // SUB
            == lax.broadcasted_iota(jnp.int32, (big, n), 1)).astype(BF16)
    spread = jnp.dot(pick, cross_mix[...], preferred_element_type=F32).astype(BF16)
    spread = lax.dot_general(spread, pick, (((1,), (1,)), ((), ())), preferred_element_type=F32)
    same = (lax.broadcasted_iota(jnp.int32, (big, big), 0) % SUB
            == lax.broadcasted_iota(jnp.int32, (big, big), 1) % SUB)
    kron[...] = jnp.where(same, spread, 0.0).astype(BF16)

    tile = 32

    @pl.loop(0, CHUNKS)
    def _(g):
        load(g).wait()

        @pl.loop(0, part // tile)
        def _(i):
            at_rows = pl.ds(pl.multiple_of(g * part + i * tile, tile), tile)
            raw = tok[at_rows, :].astype(F32)
            mean_square = jnp.mean(raw * raw, axis=-1, keepdims=True)
            normed[at_rows, :] = (raw * lax.rsqrt(mean_square + 1e-06) * gain_mix[...]).astype(BF16)

    load_mat.wait()
    line_arrived(0)
    for t in range(1, 2):
        line_start(t)

    bits = []
    while (1 << len(bits)) < n:
        b = 1 << len(bits)
        bits.append((b, (1 - 2 * ((me // b) % 2)) * b))

    def partner(k):
        q = me
        for b, step in bits:
            q = q + ((k // b) % 2) * step
        return q

    def exchange(src, dst, g, send_sem, recv_sem):
        pltpu.make_async_copy(src.at[g, me], dst.at[g, me], recv_sem.at[g]).start()

        @pl.loop(1, n)
        def _(k):
            q = partner(n - k)
            pltpu.make_async_remote_copy(
                src_ref=src.at[g, q], dst_ref=dst.at[g, me],
                send_sem=send_sem.at[g], recv_sem=recv_sem.at[g],
                device_id=(x, q), device_id_type=MESH,
            ).start()

    def wait_all(ref, g, sem):
        pltpu.make_async_copy(ref.at[g], ref.at[g], sem.at[g]).wait()

    def wait_sent(ref, g, sem):
        block = ref.at[g, pl.ds(0, n - 1)]
        pltpu.make_async_copy(block, block, sem.at[g]).wait()

    def mix_positions(g):
        left = mat[rows_of(g), :]

        @pl.loop(0, width // 256)
        def _(j):
            res = jnp.dot(left, normed[:, pl.ds(pl.multiple_of(j * 256, 256), 256)],
                          preferred_element_type=F32).astype(BF16)
            for r in range(row_groups):
                for c in range(2):
                    send1[g, r * col_groups + 2 * j + c] = res[
                        r * rows:(r + 1) * rows, c * LANES:(c + 1) * LANES]
        exchange(send1, got1, g, s1, r1)

    def weights_2():
        for t in range(1, line - 1):
            line_arrived(t)
            if t + 1 < line - 1:
                line_start(t + 1)

    def weights_3():
        by_kind(lambda _, full: hop(full, lane, 0, peer_y).start())

    def weights_4():
        by_kind(lambda _, full: arrived(full, over_y, 0))

        def go(_, full):
            hop(full, lane, 1, peer_x).start()
            hop(full, over_y, 2, peer_x).start()
        by_kind(go)

    def from_x(x_kind):
        full = wout if x_kind == 0 else win
        arrived(full, lane, 1)
        arrived(full, over_y, 2)

    def weights_5():
        @pl.when(x == 0)
        def _():
            from_x(0)

        @pl.when(x == 1)
        def _():
            from_x(1)
        hop(win, lane, 3, peer_c).start()
        hop(win, over_y, 4, peer_c).start()
        hop(wout, lane, 5, peer_c).start()
        hop(wout, over_y, 6, peer_c).start()

    @pl.loop(0, CHUNKS)
    def _(g):
        mix_positions(g)
        pl.when(g == 1)(weights_2)
        pl.when(g == 2)(weights_3)
        pl.when(g == 5)(weights_4)

    pair = 2 if rows % (2 * SUB) == 0 else 1

    @pl.loop(0, CHUNKS)
    def _(g):
        wait_all(got1, g, r1)
        for t in range(rows // (SUB * pair)):
            cuts = [slice((t * pair + p) * SUB, (t * pair + p + 1) * SUB) for p in range(pair)]
            parts = [got1[g, :, cut, :].reshape(big, LANES) for cut in cuts]
            joined = parts[0] if pair == 1 else jnp.concatenate(parts, axis=1)
            res = jnp.dot(kron[...], joined, preferred_element_type=F32).astype(BF16)
            for p in range(pair):
                send2[g, :, cuts[p], :] = res[:, p * LANES:(p + 1) * LANES].reshape(n, SUB, LANES)
        exchange(send2, got2, g, s2, r2)
        pl.when(g == 2)(weights_5)

    arrived(win, over_c, 3)
    arrived(win, over_yc, 4)
    arrived(wout, over_c, 5)
    arrived(wout, over_yc, 6)

    depth = width // NCB
    hidden_width = w_in.shape[-1]
    per = line // NCB
    small = min(rows, 32)

    def store(g):
        return pltpu.make_async_copy(result.at[rows_of(g)], out.at[rows_of(g)], out_sem.at[g])

    @pl.loop(0, CHUNKS)
    def _(g):
        wait_all(got2, g, r2)

        for i in range(part // small):
            r, inside = divmod(i * small, rows)
            cut = slice(i * small, (i + 1) * small)
            at_rows = pl.ds(pl.multiple_of(g * part + i * small, small), small)
            mixed = jnp.concatenate(
                [got2[g, r * col_groups + c, inside:inside + small, :] for c in range(col_groups)], axis=1)
            gate = (tok[at_rows, :].astype(F32)
                    + normed[at_rows, :].astype(F32) * mixed.astype(F32)).astype(BF16)
            gated[cut, :] = gate
            wide = gate.astype(F32)
            mean_square = jnp.mean(wide * wide, axis=-1, keepdims=True)
            inner[cut, :] = (wide * lax.rsqrt(mean_square + 1e-06) * gain_mlp[...]).astype(BF16)

        for b in range(NCB):
            cols = slice(b * depth, (b + 1) * depth)
            first = win[b * per:(b + 1) * per].reshape(depth, hidden_width)
            hidden = jnp.dot(inner[:, cols], first, preferred_element_type=F32)
            hidden = jax.nn.gelu(hidden).astype(BF16)
            second = wout[b * per:(b + 1) * per].reshape(hidden_width, depth)
            res = jnp.dot(hidden, second, preferred_element_type=F32)
            result[rows_of(g), cols] = (gated[:, cols].astype(F32) + res).astype(BF16)
        store(g).start()

    for t in range(line - 1):
        line_sent(t)
    by_kind(lambda _, full: hop(full, lane, 0, peer_y).wait_send())

    def sent_x(_, full):
        hop(full, lane, 1, peer_x).wait_send()
        hop(full, over_y, 2, peer_x).wait_send()
    by_kind(sent_x)
    hop(win, lane, 3, peer_c).wait_send()
    hop(win, over_y, 4, peer_c).wait_send()
    hop(wout, lane, 5, peer_c).wait_send()
    hop(wout, over_y, 6, peer_c).wait_send()

    @pl.loop(0, CHUNKS)
    def _(g):
        wait_sent(send1, g, s1)
        wait_sent(send2, g, s2)
        store(g).wait()


def make(n):
    def shards(tokens, gain_mix, gain_mlp, block_mix, cross_mix, w_in, w_out):
        count, width = tokens.shape
        part = BLK // CHUNKS
        rows = part // (n // (width // LANES))
        line = n // 4
        vmem = pl.BlockSpec(memory_space=pltpu.VMEM)
        hbm = pl.BlockSpec(memory_space=pl.ANY)
        dma = pltpu.SemaphoreType.DMA
        block = pltpu.VMEM((CHUNKS, n, rows, LANES), BF16)
        whole = pltpu.VMEM((count, width), BF16)
        def body(*refs):
            kernel(n, *refs)
        return pl.pallas_call(
            body,
            out_shape=jax.ShapeDtypeStruct((count, width), BF16),
            in_specs=[hbm, vmem, vmem, hbm, vmem, hbm, hbm],
            out_specs=hbm,
            scratch_shapes=[
                whole, whole, pltpu.VMEM((BLK, BLK), BF16),
                pltpu.VMEM((line, 4) + w_in.shape, BF16),
                pltpu.VMEM((line, 4) + w_out.shape, BF16),
                block, block, block, block,
                pltpu.VMEM((n * SUB, n * SUB), BF16),
                pltpu.VMEM((part, width), BF16), pltpu.VMEM((part, width), BF16), whole,
                dma((CHUNKS,)), dma(()), dma(()), dma((2, line)), dma((2, line)), dma((7,)), dma((7,)),
                dma((CHUNKS,)), dma((CHUNKS,)), dma((CHUNKS,)), dma((CHUNKS,)), dma((CHUNKS,)),
            ],
            compiler_params=pltpu.CompilerParams(
                collective_id=0, has_side_effects=True, vmem_limit_bytes=58 * 1024 * 1024),
        )(tokens, gain_mix.reshape(1, -1), gain_mlp.reshape(1, -1), block_mix, cross_mix, w_in, w_out)
    return shards


def solution(mesh):
    in_specs = (P(("groups", "seq"), None), P(), P(), P(), P(), P("seq", None), P("seq", None))
    out_specs = P(("groups", "seq"), None)
    return jax.shard_map(make(mesh.shape["seq"]), mesh=mesh, in_specs=in_specs, out_specs=out_specs, check_vma=False)
```

```python
import jax
import jax.numpy as jnp
from jax import lax
from jax.experimental import pallas as pl
from jax.experimental.pallas import tpu as pltpu
from jax.sharding import PartitionSpec as P

NCB = 4
BLK = 1024
CHUNKS = 8
LANES = 128
SUB = 16
MESH = pl.DeviceIdType.MESH
BF16 = jnp.bfloat16
F32 = jnp.float32


def kernel(
    n, tokens, gain_mix, gain_mlp, block_mix, cross_mix, w_in, w_out, out,
    tok, normed, mat, win, wout, send1, got1, send2, got2, kron, gated, inner, result,
    load_sem, mat_sem, own_sem, line_send, line_recv, hop_send, hop_recv,
    s1, r1, s2, r2, out_sem,
):
    width = tokens.shape[1]
    part = BLK // CHUNKS
    col_groups = width // LANES
    row_groups = n // col_groups
    rows = part // row_groups
    line = n // 4
    x = lax.axis_index("groups")
    me = lax.axis_index("seq")
    at, lane = me // 4, me % 4
    y, core = lane // 2, lane % 2

    def rows_of(g):
        return pl.ds(pl.multiple_of(g * part, part), part)

    def load(g):
        return pltpu.make_async_copy(tokens.at[rows_of(g)], tok.at[rows_of(g)], load_sem.at[g])

    barrier = pltpu.get_barrier_semaphore()

    @pl.loop(1, n)
    def _(k):
        pl.semaphore_signal(barrier, inc=1, device_id=(x, (me + k) % n), device_id_type=MESH)

    pl.semaphore_signal(barrier, inc=1, device_id=(1 - x, me), device_id_type=MESH)
    @pl.loop(0, CHUNKS)
    def _(g):
        load(g).start()

    load_mat = pltpu.make_async_copy(block_mix, mat, mat_sem)
    load_mat.start()


    def by_kind(fn):
        @pl.when(x == 0)
        def _():
            fn(w_in, win)

        @pl.when(x == 1)
        def _():
            fn(w_out, wout)

    def line_copy(mine, full, t, way):
        shard = at - t if way == 0 else at + t
        to = at + 1 if way == 0 else at - 1
        return pltpu.make_async_remote_copy(
            src_ref=mine if t == 0 else full.at[shard, lane], dst_ref=full.at[shard, lane],
            send_sem=line_send.at[way, t], recv_sem=line_recv.at[way, t],
            device_id=(x, to * 4 + lane), device_id_type=MESH,
        )

    def line_start(t):
        def go(mine, full):
            @pl.when((at < line - 1) & (at - t >= 0))
            def _():
                line_copy(mine, full, t, 0).start()

            @pl.when((at > 0) & (at + t <= line - 1))
            def _():
                line_copy(mine, full, t, 1).start()
        by_kind(go)

    def line_arrived(t):
        def go(_, full):
            @pl.when(at - 1 - t >= 0)
            def _():
                block = full.at[at - 1 - t, lane]
                pltpu.make_async_copy(block, block, line_recv.at[0, t]).wait()

            @pl.when(at + 1 + t <= line - 1)
            def _():
                block = full.at[at + 1 + t, lane]
                pltpu.make_async_copy(block, block, line_recv.at[1, t]).wait()
        by_kind(go)

    def line_sent(t):
        def go(mine, full):
            @pl.when((at < line - 1) & (at - t >= 0))
            def _():
                line_copy(mine, full, t, 0).wait_send()

            @pl.when((at > 0) & (at + t <= line - 1))
            def _():
                line_copy(mine, full, t, 1).wait_send()
        by_kind(go)

    def hop(full, which, slot, device):
        return pltpu.make_async_remote_copy(
            src_ref=full.at[:, which], dst_ref=full.at[:, which],
            send_sem=hop_send.at[slot], recv_sem=hop_recv.at[slot],
            device_id=device, device_id_type=MESH,
        )

    def arrived(full, which, slot):
        block = full.at[:, which]
        pltpu.make_async_copy(block, block, hop_recv.at[slot]).wait()

    over_y = (1 - y) * 2 + core
    over_c = y * 2 + 1 - core
    over_yc = (1 - y) * 2 + 1 - core
    peer_y = (x, at * 4 + over_y)
    peer_x = (1 - x, me)
    peer_c = (x, at * 4 + over_c)

    def own(shard, full):
        return pltpu.make_async_copy(shard, full.at[at, lane], own_sem)

    big = n * SUB
    pick = (lax.broadcasted_iota(jnp.int32, (big, n), 0) // SUB
            == lax.broadcasted_iota(jnp.int32, (big, n), 1)).astype(BF16)
    spread = jnp.dot(pick, cross_mix[...], preferred_element_type=F32).astype(BF16)
    spread = lax.dot_general(spread, pick, (((1,), (1,)), ((), ())), preferred_element_type=F32)
    same = (lax.broadcasted_iota(jnp.int32, (big, big), 0) % SUB
            == lax.broadcasted_iota(jnp.int32, (big, big), 1) % SUB)
    kron[...] = jnp.where(same, spread, 0.0).astype(BF16)

    pl.semaphore_wait(barrier, n)
    by_kind(lambda shard, full: own(shard, full).start())
    line_start(0)

    tile = 32

    @pl.loop(0, CHUNKS)
    def _(g):
        load(g).wait()

        @pl.loop(0, part // tile)
        def _(i):
            at_rows = pl.ds(pl.multiple_of(g * part + i * tile, tile), tile)
            raw = tok[at_rows, :].astype(F32)
            mean_square = jnp.mean(raw * raw, axis=-1, keepdims=True)
            normed[at_rows, :] = (raw * lax.rsqrt(mean_square + 1e-06) * gain_mix[...]).astype(BF16)

    load_mat.wait()

    bits = []
    while (1 << len(bits)) < n:
        b = 1 << len(bits)
        bits.append((b, (1 - 2 * ((me // b) % 2)) * b))

    def partner(k):
        q = me
        for b, step in bits:
            q = q + ((k // b) % 2) * step
        return q

    def exchange(src, dst, g, send_sem, recv_sem):
        pltpu.make_async_copy(src.at[g, me], dst.at[g, me], recv_sem.at[g]).start()

        @pl.loop(1, n)
        def _(k):
            q = partner(k)
            pltpu.make_async_remote_copy(
                src_ref=src.at[g, q], dst_ref=dst.at[g, me],
                send_sem=send_sem.at[g], recv_sem=recv_sem.at[g],
                device_id=(x, q), device_id_type=MESH,
            ).start()

    def wait_all(ref, g, sem):
        pltpu.make_async_copy(ref.at[g], ref.at[g], sem.at[g]).wait()

    def wait_sent(ref, g, sem):
        block = ref.at[g, pl.ds(0, n - 1)]
        pltpu.make_async_copy(block, block, sem.at[g]).wait()

    def mix_positions(g):
        left = mat[rows_of(g), :]

        @pl.loop(0, width // 256)
        def _(j):
            res = jnp.dot(left, normed[:, pl.ds(pl.multiple_of(j * 256, 256), 256)],
                          preferred_element_type=F32).astype(BF16)
            for r in range(row_groups):
                for c in range(2):
                    send1[g, r * col_groups + 2 * j + c] = res[
                        r * rows:(r + 1) * rows, c * LANES:(c + 1) * LANES]
        exchange(send1, got1, g, s1, r1)

    def weights_2():
        for t in range(1, line - 1):
            line_arrived(t)
            if t + 1 < line - 1:
                line_start(t + 1)

    def weights_3():
        by_kind(lambda shard, full: own(shard, full).wait())
        by_kind(lambda _, full: hop(full, lane, 0, peer_y).start())

    def weights_4():
        by_kind(lambda _, full: arrived(full, over_y, 0))

        def go(_, full):
            hop(full, lane, 1, peer_x).start()
            hop(full, over_y, 2, peer_x).start()
        by_kind(go)

    def from_x(x_kind):
        full = wout if x_kind == 0 else win
        arrived(full, lane, 1)
        arrived(full, over_y, 2)

    def weights_5():
        @pl.when(x == 0)
        def _():
            from_x(0)

        @pl.when(x == 1)
        def _():
            from_x(1)
        hop(win, lane, 3, peer_c).start()
        hop(win, over_y, 4, peer_c).start()
        hop(wout, lane, 5, peer_c).start()
        hop(wout, over_y, 6, peer_c).start()

    @pl.loop(0, CHUNKS)
    def _(g):
        mix_positions(g)

        @pl.when(g == 0)
        def _():
            line_arrived(0)
            line_start(1)

        @pl.when(g == 1)
        def _():
            weights_2()
            weights_3()

    pair = 2 if rows % (2 * SUB) == 0 else 1

    @pl.loop(0, CHUNKS)
    def _(g):
        wait_all(got1, g, r1)
        for t in range(rows // (SUB * pair)):
            cuts = [slice((t * pair + p) * SUB, (t * pair + p + 1) * SUB) for p in range(pair)]
            parts = [got1[g, :, cut, :].reshape(big, LANES) for cut in cuts]
            joined = parts[0] if pair == 1 else jnp.concatenate(parts, axis=1)
            res = jnp.dot(kron[...], joined, preferred_element_type=F32).astype(BF16)
            for p in range(pair):
                send2[g, :, cuts[p], :] = res[:, p * LANES:(p + 1) * LANES].reshape(n, SUB, LANES)
        exchange(send2, got2, g, s2, r2)
        pl.when(g == 0)(weights_4)
        pl.when(g == CHUNKS // 2)(weights_5)

    arrived(win, over_c, 3)
    arrived(win, over_yc, 4)
    arrived(wout, over_c, 5)
    arrived(wout, over_yc, 6)

    depth = width // NCB
    hidden_width = w_in.shape[-1]
    per = line // NCB
    small = min(rows, 32)

    def store(g):
        return pltpu.make_async_copy(result.at[rows_of(g)], out.at[rows_of(g)], out_sem.at[g])

    @pl.loop(0, CHUNKS)
    def _(g):
        wait_all(got2, g, r2)

        for i in range(part // small):
            r, inside = divmod(i * small, rows)
            cut = slice(i * small, (i + 1) * small)
            at_rows = pl.ds(pl.multiple_of(g * part + i * small, small), small)
            mixed = jnp.concatenate(
                [got2[g, r * col_groups + c, inside:inside + small, :] for c in range(col_groups)], axis=1)
            gate = (tok[at_rows, :].astype(F32)
                    + normed[at_rows, :].astype(F32) * mixed.astype(F32)).astype(BF16)
            gated[cut, :] = gate
            wide = gate.astype(F32)
            mean_square = jnp.mean(wide * wide, axis=-1, keepdims=True)
            inner[cut, :] = (wide * lax.rsqrt(mean_square + 1e-06) * gain_mlp[...]).astype(BF16)

        for b in range(NCB):
            cols = slice(b * depth, (b + 1) * depth)
            first = win[b * per:(b + 1) * per].reshape(depth, hidden_width)
            hidden = jnp.dot(inner[:, cols], first, preferred_element_type=F32)
            hidden = jax.nn.gelu(hidden).astype(BF16)
            second = wout[b * per:(b + 1) * per].reshape(hidden_width, depth)
            res = jnp.dot(hidden, second, preferred_element_type=F32)
            result[rows_of(g), cols] = (gated[:, cols].astype(F32) + res).astype(BF16)
        store(g).start()

    for t in range(line - 1):
        line_sent(t)
    by_kind(lambda _, full: hop(full, lane, 0, peer_y).wait_send())

    def sent_x(_, full):
        hop(full, lane, 1, peer_x).wait_send()
        hop(full, over_y, 2, peer_x).wait_send()
    by_kind(sent_x)
    hop(win, lane, 3, peer_c).wait_send()
    hop(win, over_y, 4, peer_c).wait_send()
    hop(wout, lane, 5, peer_c).wait_send()
    hop(wout, over_y, 6, peer_c).wait_send()

    @pl.loop(0, CHUNKS)
    def _(g):
        wait_sent(send1, g, s1)
        wait_sent(send2, g, s2)
        store(g).wait()


def write_out(result, out, in_sem, out_sem, held):
    part = result.shape[0] // CHUNKS
    cuts = [pl.ds(g * part, part) for g in range(CHUNKS)]
    for g, cut in enumerate(cuts):
        pltpu.make_async_copy(result.at[cut], held.at[cut], in_sem.at[g]).start()
    for g, cut in enumerate(cuts):
        pltpu.make_async_copy(result.at[cut], held.at[cut], in_sem.at[g]).wait()
        pltpu.make_async_copy(held.at[cut], out.at[cut], out_sem.at[g]).start()
    for g, cut in enumerate(cuts):
        pltpu.make_async_copy(held.at[cut], out.at[cut], out_sem.at[g]).wait()


def make(n):
    def shards(tokens, gain_mix, gain_mlp, block_mix, cross_mix, w_in, w_out):
        count, width = tokens.shape
        part = BLK // CHUNKS
        rows = part // (n // (width // LANES))
        line = n // 4
        vmem = pl.BlockSpec(memory_space=pltpu.VMEM)
        hbm = pl.BlockSpec(memory_space=pl.ANY)
        dma = pltpu.SemaphoreType.DMA
        block = pltpu.VMEM((CHUNKS, n, rows, LANES), BF16)
        whole = pltpu.VMEM((count, width), BF16)
        def body(*refs):
            kernel(n, *refs)
        result = pl.pallas_call(
            body,
            out_shape=jax.ShapeDtypeStruct((count, width), BF16),
            in_specs=[hbm, vmem, vmem, hbm, vmem, hbm, hbm],
            out_specs=hbm,
            scratch_shapes=[
                whole, whole, pltpu.VMEM((BLK, BLK), BF16),
                pltpu.VMEM((line, 4) + w_in.shape, BF16),
                pltpu.VMEM((line, 4) + w_out.shape, BF16),
                block, block, block, block,
                pltpu.VMEM((n * SUB, n * SUB), BF16),
                pltpu.VMEM((part, width), BF16), pltpu.VMEM((part, width), BF16), whole,
                dma((CHUNKS,)), dma(()), dma(()), dma((2, line)), dma((2, line)), dma((7,)), dma((7,)),
                dma((CHUNKS,)), dma((CHUNKS,)), dma((CHUNKS,)), dma((CHUNKS,)), dma((CHUNKS,)),
            ],
            compiler_params=pltpu.CompilerParams(
                collective_id=0, has_side_effects=True, vmem_limit_bytes=58 * 1024 * 1024),
        )(tokens, gain_mix.reshape(1, -1), gain_mlp.reshape(1, -1), block_mix, cross_mix, w_in, w_out)
        return pl.pallas_call(
            write_out,
            out_shape=jax.ShapeDtypeStruct((count, width), BF16),
            in_specs=[hbm],
            out_specs=hbm,
            scratch_shapes=[dma((CHUNKS,)), dma((CHUNKS,)), whole],
            compiler_params=pltpu.CompilerParams(vmem_limit_bytes=16 * 1024 * 1024),
        )(result)
    return shards


def solution(mesh):
    in_specs = (P(("groups", "seq"), None), P(), P(), P(), P(), P("seq", None), P("seq", None))
    out_specs = P(("groups", "seq"), None)
    return jax.shard_map(make(mesh.shape["seq"]), mesh=mesh, in_specs=in_specs, out_specs=out_specs, check_vma=False)
```

```python
import jax
import jax.numpy as jnp
from jax import lax
from jax.experimental import pallas as pl
from jax.experimental.pallas import tpu as pltpu
from jax.sharding import PartitionSpec as P

NCB = 4
BLK = 1024
CHUNKS = 8
LANES = 128
SUB = 16
MESH = pl.DeviceIdType.MESH
BF16 = jnp.bfloat16
F32 = jnp.float32


def kernel(
    n, tokens, gain_mix, gain_mlp, block_mix, cross_mix, w_in, w_out, out,
    tok, normed, mat, win, wout, send1, got1, send2, got2, kron, gated, inner, result,
    load_sem, mat_sem, own_sem, line_send, line_recv, hop_send, hop_recv,
    s1, r1, s2, r2, out_sem,
):
    width = tokens.shape[1]
    part = BLK // CHUNKS
    col_groups = width // LANES
    row_groups = n // col_groups
    rows = part // row_groups
    line = n // 4
    x = lax.axis_index("groups")
    me = lax.axis_index("seq")
    at, lane = me // 4, me % 4
    y, core = lane // 2, lane % 2

    def rows_of(g):
        return pl.ds(pl.multiple_of(g * part, part), part)

    def load(g):
        return pltpu.make_async_copy(tokens.at[rows_of(g)], tok.at[rows_of(g)], load_sem.at[g])

    barrier = pltpu.get_barrier_semaphore()

    @pl.loop(1, n)
    def _(k):
        pl.semaphore_signal(barrier, inc=1, device_id=(x, (me + k) % n), device_id_type=MESH)

    pl.semaphore_signal(barrier, inc=1, device_id=(1 - x, me), device_id_type=MESH)
    @pl.loop(0, CHUNKS)
    def _(g):
        load(g).start()

    load_mat = pltpu.make_async_copy(block_mix, mat, mat_sem)
    load_mat.start()


    def by_kind(fn):
        @pl.when(x == 0)
        def _():
            fn(w_in, win)

        @pl.when(x == 1)
        def _():
            fn(w_out, wout)

    def line_copy(mine, full, t, way):
        shard = at - t if way == 0 else at + t
        to = at + 1 if way == 0 else at - 1
        return pltpu.make_async_remote_copy(
            src_ref=mine if t == 0 else full.at[shard, lane], dst_ref=full.at[shard, lane],
            send_sem=line_send.at[way, t], recv_sem=line_recv.at[way, t],
            device_id=(x, to * 4 + lane), device_id_type=MESH,
        )

    def line_start(t):
        def go(mine, full):
            @pl.when((at < line - 1) & (at - t >= 0))
            def _():
                line_copy(mine, full, t, 0).start()

            @pl.when((at > 0) & (at + t <= line - 1))
            def _():
                line_copy(mine, full, t, 1).start()
        by_kind(go)

    def line_arrived(t):
        def go(_, full):
            @pl.when(at - 1 - t >= 0)
            def _():
                block = full.at[at - 1 - t, lane]
                pltpu.make_async_copy(block, block, line_recv.at[0, t]).wait()

            @pl.when(at + 1 + t <= line - 1)
            def _():
                block = full.at[at + 1 + t, lane]
                pltpu.make_async_copy(block, block, line_recv.at[1, t]).wait()
        by_kind(go)

    def line_sent(t):
        def go(mine, full):
            @pl.when((at < line - 1) & (at - t >= 0))
            def _():
                line_copy(mine, full, t, 0).wait_send()

            @pl.when((at > 0) & (at + t <= line - 1))
            def _():
                line_copy(mine, full, t, 1).wait_send()
        by_kind(go)

    def hop(full, which, slot, device):
        return pltpu.make_async_remote_copy(
            src_ref=full.at[:, which], dst_ref=full.at[:, which],
            send_sem=hop_send.at[slot], recv_sem=hop_recv.at[slot],
            device_id=device, device_id_type=MESH,
        )

    def arrived(full, which, slot):
        block = full.at[:, which]
        pltpu.make_async_copy(block, block, hop_recv.at[slot]).wait()

    over_y = (1 - y) * 2 + core
    over_c = y * 2 + 1 - core
    over_yc = (1 - y) * 2 + 1 - core
    peer_y = (x, at * 4 + over_y)
    peer_x = (1 - x, me)
    peer_c = (x, at * 4 + over_c)

    def own(shard, full):
        return pltpu.make_async_copy(shard, full.at[at, lane], own_sem)

    big = n * SUB
    pick = (lax.broadcasted_iota(jnp.int32, (big, n), 0) // SUB
            == lax.broadcasted_iota(jnp.int32, (big, n), 1)).astype(BF16)
    spread = jnp.dot(pick, cross_mix[...], preferred_element_type=F32).astype(BF16)
    spread = lax.dot_general(spread, pick, (((1,), (1,)), ((), ())), preferred_element_type=F32)
    same = (lax.broadcasted_iota(jnp.int32, (big, big), 0) % SUB
            == lax.broadcasted_iota(jnp.int32, (big, big), 1) % SUB)
    kron[...] = jnp.where(same, spread, 0.0).astype(BF16)

    tile = 32

    @pl.loop(0, CHUNKS)
    def _(g):
        load(g).wait()

        @pl.loop(0, part // tile)
        def _(i):
            at_rows = pl.ds(pl.multiple_of(g * part + i * tile, tile), tile)
            raw = tok[at_rows, :].astype(F32)
            mean_square = jnp.mean(raw * raw, axis=-1, keepdims=True)
            normed[at_rows, :] = (raw * lax.rsqrt(mean_square + 1e-06) * gain_mix[...]).astype(BF16)

    pl.semaphore_wait(barrier, n)
    by_kind(lambda shard, full: own(shard, full).start())
    line_start(0)
    load_mat.wait()

    bits = []
    while (1 << len(bits)) < n:
        b = 1 << len(bits)
        bits.append((b, (1 - 2 * ((me // b) % 2)) * b))

    def partner(k):
        q = me
        for b, step in bits:
            q = q + ((k // b) % 2) * step
        return q

    def exchange(src, dst, g, send_sem, recv_sem):
        pltpu.make_async_copy(src.at[g, me], dst.at[g, me], recv_sem.at[g]).start()

        @pl.loop(1, n)
        def _(k):
            q = partner(k)
            pltpu.make_async_remote_copy(
                src_ref=src.at[g, q], dst_ref=dst.at[g, me],
                send_sem=send_sem.at[g], recv_sem=recv_sem.at[g],
                device_id=(x, q), device_id_type=MESH,
            ).start()

    def wait_all(ref, g, sem):
        pltpu.make_async_copy(ref.at[g], ref.at[g], sem.at[g]).wait()

    def wait_sent(ref, g, sem):
        block = ref.at[g, pl.ds(0, n - 1)]
        pltpu.make_async_copy(block, block, sem.at[g]).wait()

    def mix_positions(g):
        left = mat[rows_of(g), :]

        @pl.loop(0, width // 256)
        def _(j):
            res = jnp.dot(left, normed[:, pl.ds(pl.multiple_of(j * 256, 256), 256)],
                          preferred_element_type=F32).astype(BF16)
            for r in range(row_groups):
                for c in range(2):
                    send1[g, r * col_groups + 2 * j + c] = res[
                        r * rows:(r + 1) * rows, c * LANES:(c + 1) * LANES]
        exchange(send1, got1, g, s1, r1)

    def weights_2():
        for t in range(1, line - 1):
            line_arrived(t)
            if t + 1 < line - 1:
                line_start(t + 1)

    def weights_3():
        by_kind(lambda shard, full: own(shard, full).wait())
        by_kind(lambda _, full: hop(full, lane, 0, peer_y).start())

    def weights_4():
        by_kind(lambda _, full: arrived(full, over_y, 0))

        def go(_, full):
            hop(full, lane, 1, peer_x).start()
            hop(full, over_y, 2, peer_x).start()
        by_kind(go)

    def from_x(x_kind):
        full = wout if x_kind == 0 else win
        arrived(full, lane, 1)
        arrived(full, over_y, 2)

    def weights_5():
        @pl.when(x == 0)
        def _():
            from_x(0)

        @pl.when(x == 1)
        def _():
            from_x(1)
        hop(win, lane, 3, peer_c).start()
        hop(win, over_y, 4, peer_c).start()
        hop(wout, lane, 5, peer_c).start()
        hop(wout, over_y, 6, peer_c).start()

    @pl.loop(0, CHUNKS)
    def _(g):
        mix_positions(g)

        @pl.when(g == 0)
        def _():
            line_arrived(0)
            line_start(1)

        @pl.when(g == 1)
        def _():
            weights_2()
            weights_3()

    pair = 2 if rows % (2 * SUB) == 0 else 1

    @pl.loop(0, CHUNKS)
    def _(g):
        wait_all(got1, g, r1)
        for t in range(rows // (SUB * pair)):
            cuts = [slice((t * pair + p) * SUB, (t * pair + p + 1) * SUB) for p in range(pair)]
            parts = [got1[g, :, cut, :].reshape(big, LANES) for cut in cuts]
            joined = parts[0] if pair == 1 else jnp.concatenate(parts, axis=1)
            res = jnp.dot(kron[...], joined, preferred_element_type=F32).astype(BF16)
            for p in range(pair):
                send2[g, :, cuts[p], :] = res[:, p * LANES:(p + 1) * LANES].reshape(n, SUB, LANES)
        exchange(send2, got2, g, s2, r2)
        pl.when(g == 0)(weights_4)
        pl.when(g == CHUNKS // 2)(weights_5)

    arrived(win, over_c, 3)
    arrived(win, over_yc, 4)
    arrived(wout, over_c, 5)
    arrived(wout, over_yc, 6)

    depth = width // NCB
    hidden_width = w_in.shape[-1]
    per = line // NCB
    small = min(rows, 32)

    def store(g):
        return pltpu.make_async_copy(result.at[rows_of(g)], out.at[rows_of(g)], out_sem.at[g])

    @pl.loop(0, CHUNKS)
    def _(g):
        wait_all(got2, g, r2)

        for i in range(part // small):
            r, inside = divmod(i * small, rows)
            cut = slice(i * small, (i + 1) * small)
            at_rows = pl.ds(pl.multiple_of(g * part + i * small, small), small)
            mixed = jnp.concatenate(
                [got2[g, r * col_groups + c, inside:inside + small, :] for c in range(col_groups)], axis=1)
            gate = (tok[at_rows, :].astype(F32)
                    + normed[at_rows, :].astype(F32) * mixed.astype(F32)).astype(BF16)
            gated[cut, :] = gate
            wide = gate.astype(F32)
            mean_square = jnp.mean(wide * wide, axis=-1, keepdims=True)
            inner[cut, :] = (wide * lax.rsqrt(mean_square + 1e-06) * gain_mlp[...]).astype(BF16)

        for b in range(NCB):
            cols = slice(b * depth, (b + 1) * depth)
            first = win[b * per:(b + 1) * per].reshape(depth, hidden_width)
            hidden = jnp.dot(inner[:, cols], first, preferred_element_type=F32)
            hidden = jax.nn.gelu(hidden).astype(BF16)
            second = wout[b * per:(b + 1) * per].reshape(hidden_width, depth)
            res = jnp.dot(hidden, second, preferred_element_type=F32)
            result[rows_of(g), cols] = (gated[:, cols].astype(F32) + res).astype(BF16)
        store(g).start()

    for t in range(line - 1):
        line_sent(t)
    by_kind(lambda _, full: hop(full, lane, 0, peer_y).wait_send())

    def sent_x(_, full):
        hop(full, lane, 1, peer_x).wait_send()
        hop(full, over_y, 2, peer_x).wait_send()
    by_kind(sent_x)
    hop(win, lane, 3, peer_c).wait_send()
    hop(win, over_y, 4, peer_c).wait_send()
    hop(wout, lane, 5, peer_c).wait_send()
    hop(wout, over_y, 6, peer_c).wait_send()

    @pl.loop(0, CHUNKS)
    def _(g):
        wait_sent(send1, g, s1)
        wait_sent(send2, g, s2)
        store(g).wait()


def write_out(result, out, in_sem, out_sem, held):
    part = result.shape[0] // CHUNKS
    cuts = [pl.ds(g * part, part) for g in range(CHUNKS)]
    for g, cut in enumerate(cuts):
        pltpu.make_async_copy(result.at[cut], held.at[cut], in_sem.at[g]).start()
    for g, cut in enumerate(cuts):
        pltpu.make_async_copy(result.at[cut], held.at[cut], in_sem.at[g]).wait()
        pltpu.make_async_copy(held.at[cut], out.at[cut], out_sem.at[g]).start()
    for g, cut in enumerate(cuts):
        pltpu.make_async_copy(held.at[cut], out.at[cut], out_sem.at[g]).wait()


def make(n):
    def shards(tokens, gain_mix, gain_mlp, block_mix, cross_mix, w_in, w_out):
        count, width = tokens.shape
        part = BLK // CHUNKS
        rows = part // (n // (width // LANES))
        line = n // 4
        vmem = pl.BlockSpec(memory_space=pltpu.VMEM)
        hbm = pl.BlockSpec(memory_space=pl.ANY)
        dma = pltpu.SemaphoreType.DMA
        block = pltpu.VMEM((CHUNKS, n, rows, LANES), BF16)
        whole = pltpu.VMEM((count, width), BF16)
        def body(*refs):
            kernel(n, *refs)
        result = pl.pallas_call(
            body,
            out_shape=jax.ShapeDtypeStruct((count, width), BF16),
            in_specs=[hbm, vmem, vmem, hbm, vmem, hbm, hbm],
            out_specs=hbm,
            scratch_shapes=[
                whole, whole, pltpu.VMEM((BLK, BLK), BF16),
                pltpu.VMEM((line, 4) + w_in.shape, BF16),
                pltpu.VMEM((line, 4) + w_out.shape, BF16),
                block, block, block, block,
                pltpu.VMEM((n * SUB, n * SUB), BF16),
                pltpu.VMEM((part, width), BF16), pltpu.VMEM((part, width), BF16), whole,
                dma((CHUNKS,)), dma(()), dma(()), dma((2, line)), dma((2, line)), dma((7,)), dma((7,)),
                dma((CHUNKS,)), dma((CHUNKS,)), dma((CHUNKS,)), dma((CHUNKS,)), dma((CHUNKS,)),
            ],
            compiler_params=pltpu.CompilerParams(
                collective_id=0, has_side_effects=True, vmem_limit_bytes=58 * 1024 * 1024),
        )(tokens, gain_mix.reshape(1, -1), gain_mlp.reshape(1, -1), block_mix, cross_mix, w_in, w_out)
        return pl.pallas_call(
            write_out,
            out_shape=jax.ShapeDtypeStruct((count, width), BF16),
            in_specs=[hbm],
            out_specs=hbm,
            scratch_shapes=[dma((CHUNKS,)), dma((CHUNKS,)), whole],
            compiler_params=pltpu.CompilerParams(vmem_limit_bytes=16 * 1024 * 1024),
        )(result)
    return shards


def solution(mesh):
    in_specs = (P(("groups", "seq"), None), P(), P(), P(), P(), P("seq", None), P("seq", None))
    out_specs = P(("groups", "seq"), None)
    return jax.shard_map(make(mesh.shape["seq"]), mesh=mesh, in_specs=in_specs, out_specs=out_specs, check_vma=False)
```
